32 devices in a mesh: gr: 8 (over y, x, core), gc: 4 (over z).
Axes of the slice: x: 2, y: 2, z: 4, core: 2. Of those that a mesh axis runs over, the one named last changes fastest.
Arguments:
- queries: bfloat16 [64, 64, 8, 128], P('gr', 'gc'), may hold values from -6 to 6
- key_vectors: bfloat16 [64, 64, 8, 128], P('gr', 'gc'), may hold values from -6 to 6
- values: bfloat16 [64, 64, 8, 128], P('gr', 'gc'), may hold values from -6 to 6
- strength: bfloat16 [64, 64, 8], P('gr', 'gc'), may hold values from 0.099609375 to 0.8984375
- decay_rate: bfloat16 [64, 64, 8], P('gr', 'gc'), may hold values from 0 to 1, as said below
- out_grad: bfloat16 [64, 64, 8, 128], P('gr', 'gc'), may hold values from -6 to 6
Outputs:
- query_grad: bfloat16 [64, 64, 8, 128], P('gr', 'gc')
- key_grad: bfloat16 [64, 64, 8, 128], P('gr', 'gc')
- value_grad: bfloat16 [64, 64, 8, 128], P('gr', 'gc')
- strength_grad: bfloat16 [64, 64, 8], P('gr', 'gc')
- decay_grad: bfloat16 [64, 64, 8], P('gr', 'gc')
The draws below stay inside these ranges and needn't reach their ends.
Inputs may be any that keep to these rules, and one draw needn't show every extreme that they name: decay_rate is positive: the state keeps exp(-decay_rate) of itself at each token.
All inputs are finite; a program needn't handle non-finite values.
Results may differ from the reference program's by a relative error of at most 0.0051.
Values may be sent and summed in bfloat16 or wider, within the bound.
A program may use at most 128 MiB of HBM per device.

```python
import jax
import jax.numpy as jnp
from jax import lax

HEAD_COUNT = 8
DH = 128
GRID_HEIGHT = 64
GRID_WIDTH = 64


def draw_decay_rate(key, part):
    key = jax.random.fold_in(key, 7)
    head_seed_key, jitter_seed_key, row_seed_key, column_seed_key, spike_seed_key = jax.random.split(key, 5)
    quick_share = 0.5
    quick_heads = jax.random.uniform(head_seed_key, (HEAD_COUNT,)) < quick_share
    baseline_rate = jnp.where(quick_heads, 1.0 / 40.0, 0.3 / max(GRID_HEIGHT, GRID_WIDTH))
    jitter_level = jnp.exp(jax.random.uniform(jitter_seed_key, (GRID_HEIGHT, GRID_WIDTH, HEAD_COUNT), minval=-0.7, maxval=0.7))
    row_sweep = jnp.exp(jax.random.uniform(row_seed_key, (GRID_HEIGHT, 1, 1), minval=-0.35, maxval=0.35))
    column_sweep = jnp.exp(jax.random.uniform(column_seed_key, (1, GRID_WIDTH, 1), minval=-0.35, maxval=0.35))
    spike_events = jnp.where(jax.random.uniform(spike_seed_key, (GRID_HEIGHT, GRID_WIDTH, HEAD_COUNT)) < 1.0 / 256.0, 0.4, 0.0)
    return (baseline_rate * jitter_level * row_sweep * column_sweep + spike_events).astype(jnp.bfloat16)


def steps_of(own_key, dims, cuts, smallest, high):
    gain, own = 1.0, jax.random.fold_in(own_key, 6)
    for dim, shards_of in cuts:
        steps = jnp.exp(jax.random.uniform(jax.random.fold_in(own, dim), (shards_of,), jnp.float32, smallest / len(cuts), high / len(cuts)))
        gain = gain * jnp.repeat(steps, dims[dim] // shards_of).reshape([-1 if axis == dim else 1 for axis in range(len(dims))])
    return gain


def noise(stream_key, shape, scale, limit, cuts=(), held_as=jnp.bfloat16):
    level = steps_of(stream_key, shape, cuts, -0.22, 0.18) if cuts else 1.0
    entries = jax.random.normal(stream_key, shape, jnp.float32) * scale * level
    return jnp.minimum(jnp.maximum(entries, -limit), limit).astype(held_as)


def setup_inputs(seed: int = 0) -> dict:
    key_of = jax.random.split(jax.random.key(seed), 7)
    queries = noise(key_of[0], (GRID_HEIGHT, GRID_WIDTH, HEAD_COUNT, DH), 1.0, 6.0, ((0, 8), (1, 4)))
    key_vectors = noise(key_of[1], (GRID_HEIGHT, GRID_WIDTH, HEAD_COUNT, DH), 1.0, 6.0, ((0, 8), (1, 4)))
    values = noise(key_of[2], (GRID_HEIGHT, GRID_WIDTH, HEAD_COUNT, DH), 1.0, 6.0, ((0, 8), (1, 4)))
    strength = jnp.clip(0.099609375 + 0.7988281 * jax.random.uniform(key_of[3], (GRID_HEIGHT, GRID_WIDTH, HEAD_COUNT), jnp.float32) ** steps_of(key_of[3], (GRID_HEIGHT, GRID_WIDTH, HEAD_COUNT), ((0, 8), (1, 4)), -0.2, 0.2), 0.099609375, 0.8984375).astype(jnp.bfloat16)
    decay_rate = draw_decay_rate(jax.random.fold_in(key_of[6], 71), 0)
    out_grad = noise(key_of[5], (GRID_HEIGHT, GRID_WIDTH, HEAD_COUNT, DH), 1.0, 6.0, ((0, 8), (1, 4)))
    return {"queries": queries, "key_vectors": key_vectors, "values": values, "strength": strength, "decay_rate": decay_rate, "out_grad": out_grad}


block_len = 64
doubling_rounds = 5
highest = lax.Precision.HIGHEST

def normalize(tensor):
    return tensor / jnp.sqrt(lax.optimization_barrier(jnp.sum(tensor * tensor, axis=-1, keepdims=True)) + 1e-06)

def stretch_forward(queries, keys_in, values, gains, decays):
    length = queries.shape[0]
    lines_count = queries.shape[1]
    head_size = queries.shape[2]
    blocks_count = length // block_len

    def split_blocks(tensor):
        shaped = tensor.reshape((blocks_count, block_len) + tensor.shape[1:])
        return jnp.swapaxes(shaped, 1, 2)
    log_decay = jnp.cumsum(-split_blocks(decays), axis=-1)
    offsets = jnp.arange(block_len)
    strict = offsets[:, None] > offsets[None, :]
    inclusive = offsets[:, None] >= offsets[None, :]
    identity = jnp.eye(block_len, dtype=jnp.float32)

    def advance(state, slices):
        query_block, key_block, value_block, gain_block, decay_block = slices
        gaps = decay_block[:, :, None] - decay_block[:, None, :]
        below = jnp.where(strict, jnp.exp(jnp.where(strict, gaps, 0.0)), 0.0)
        within = jnp.where(inclusive, jnp.exp(jnp.where(inclusive, gaps, 0.0)), 0.0)
        key_key = jnp.einsum('btd,bjd->btj', key_block, key_block, precision=highest)
        lower_part = -(gain_block[:, :, None] * below * key_key)
        inverse = identity + lower_part
        power = lower_part
        for round_index in range(doubling_rounds):
            power = jnp.einsum('btj,bjs->bts', power, power, precision=highest)
            inverse = inverse + jnp.einsum('btj,bjs->bts', power, inverse, precision=highest)
        leading = jnp.exp(decay_block)[:, :, None]
        carried = jnp.einsum('btd,bde->bte', key_block, state, precision=highest)
        right_side = gain_block[:, :, None] * (value_block - leading * carried)
        writes = jnp.einsum('btj,bje->bte', inverse, right_side, precision=highest)
        query_key = jnp.einsum('btd,bjd->btj', query_block, key_block, precision=highest)
        outputs = leading * jnp.einsum('btd,bde->bte', query_block, state, precision=highest)
        outputs = outputs + jnp.einsum('btj,bje->bte', within * query_key, writes, precision=highest)
        trailing = jnp.exp(decay_block[:, -1:] - decay_block)[:, :, None]
        updated = jnp.exp(decay_block[:, -1])[:, None, None] * state
        updated = updated + jnp.einsum('bjd,bje->bde', key_block * trailing, writes, precision=highest)
        return (updated, outputs)
    state = jnp.zeros((lines_count, head_size, values.shape[-1]), jnp.float32)
    slices = (split_blocks(queries), split_blocks(keys_in), split_blocks(values), split_blocks(gains), log_decay)
    outputs = lax.scan(jax.checkpoint(advance), state, slices)[1]
    return jnp.swapaxes(outputs, 1, 2).reshape((length, lines_count, values.shape[-1]))

def directed(queries, keys_in, values, gains, decays, seq_dim):

    def as_lines(tensor):
        moved = jnp.moveaxis(tensor, seq_dim, 0)
        return moved.reshape((moved.shape[0], -1) + moved.shape[3:])
    outputs = stretch_forward(as_lines(normalize(queries)), as_lines(normalize(keys_in)), as_lines(values), as_lines(gains), as_lines(decays))
    moved_shape = jnp.moveaxis(values, seq_dim, 0).shape
    return jnp.moveaxis(outputs.reshape(moved_shape), 0, seq_dim)

def pair_grads(pieces, seq_dim):
    queries, keys_in, values, out_grad, gains, decays = pieces
    other_dim = 1 - seq_dim

    def two_ways(query_f, key_f, value_f, gain_f, decay_f):

        def both(tensor):
            return jnp.concatenate([tensor, jnp.flip(tensor, seq_dim)], axis=other_dim)
        joined = directed(both(query_f), both(key_f), both(value_f), both(gain_f), both(decay_f), seq_dim)
        half = query_f.shape[other_dim]
        forward = lax.slice_in_dim(joined, 0, half, axis=other_dim)
        backward = lax.slice_in_dim(joined, half, 2 * half, axis=other_dim)
        return forward + jnp.flip(backward, seq_dim)
    primals = tuple((tensor.astype(jnp.float32) for tensor in (queries, keys_in, values, gains, decays)))
    pullback = jax.vjp(two_ways, *primals)[1]
    gradients = pullback(out_grad.astype(jnp.float32))
    return tuple((member.astype(jnp.bfloat16) for member in gradients))

def reference(queries, key_vectors, values, strength, decay_rate, out_grad):
    pieces = (queries, key_vectors, values, out_grad, strength, decay_rate)
    row_grads = pair_grads(pieces, 1)
    column_grads = pair_grads(pieces, 0)
    merged = [(first.astype(jnp.float32) + second.astype(jnp.float32)).astype(jnp.bfloat16) for first, second in zip(row_grads, column_grads)]
    return (merged[0], merged[1], merged[2], merged[3], merged[4])
```

```python
import functools

import jax
import jax.numpy as jnp
from jax import lax
from jax.experimental import pallas as pl
from jax.experimental.pallas import tpu as pltpu
from jax.sharding import PartitionSpec as P

bf16, f32 = jnp.bfloat16, jnp.float32
lanes = 128
together = 2


def dot(a, b):
    return lax.dot_general(
        a.astype(bf16), b.astype(bf16), (((1,), (0,)), ((), ())), preferred_element_type=f32
    )


def dot_t(a, b):
    return lax.dot_general(
        a.astype(bf16), b.astype(bf16), (((1,), (1,)), ((), ())), preferred_element_type=f32
    )


def unit_inverse(x, line, apart):
    u = jnp.where(apart == 1, -x, 0.0)
    size = 2
    while size < line:
        part = jnp.where((apart >= size) & (apart < 2 * size), x, 0.0)
        left = part + dot(u, part)
        u = u - (left + dot(left, u))
        size *= 2
    return u


def solve(q, k, v, o, beta_r, decay_r, line):
    i = lax.broadcasted_iota(jnp.int32, (lanes, lanes), 0)
    j = lax.broadcasted_iota(jnp.int32, (lanes, lanes), 1)
    apart = i ^ j
    same = apart < line
    eye = apart == 0
    low, up = same & (i > j), same & (i < j)
    upto, since = same & (i >= j), same & (i <= j)
    low_m, up_m = jnp.where(low, 1.0, 0.0), jnp.where(up, 1.0, 0.0)
    upto_m, since_m = jnp.where(upto, 1.0, 0.0), jnp.where(since, 1.0, 0.0)

    kk0, qk0, kq0 = dot_t(k, k), dot_t(q, k), dot_t(k, q)
    y, yt = dot_t(o, v), dot_t(v, o)
    qf, kf = q.astype(f32), k.astype(f32)
    rq = lax.rsqrt(jnp.sum(qf * qf, axis=1, keepdims=True) + 1e-6)
    rk = lax.rsqrt(jnp.sum(kf * kf, axis=1, keepdims=True) + 1e-6)
    rq_r = jnp.sum(jnp.where(eye, rq, 0.0), axis=0, keepdims=True)
    rk_r = jnp.sum(jnp.where(eye, rk, 0.0), axis=0, keepdims=True)
    beta = dot(jnp.where(eye, beta_r, 0.0), jnp.ones((lanes, lanes), f32))
    gap = dot(jnp.where(upto, decay_r, 0.0), low_m) + dot(jnp.where(since, decay_r, 0.0), up_m)
    gap_t = dot(jnp.where(low, decay_r, 0.0), upto_m) + dot(jnp.where(up, decay_r, 0.0), since_m)
    h = jnp.where(same, jnp.exp(-gap), 0.0)
    ht = jnp.where(same, jnp.exp(-gap_t), 0.0)

    kk = kk0 * rk * rk_r
    x = kk * ht * beta_r
    uf = unit_inverse(jnp.where(up, x, 0.0), line, apart)
    ub = unit_inverse(jnp.where(low, x, 0.0), line, apart)
    pt = kq0 * rk * rq_r * ht
    ptf, ptb = jnp.where(low, 0.0, pt), jnp.where(up, 0.0, pt)
    mtf = ptf + dot(uf, ptf)
    mtb = ptb + dot(ub, ptb)
    yb = y * beta_r
    zf = yb + dot(yb, uf)
    zb = yb + dot(yb, ub)
    da = -jnp.where(low, dot(mtf, zf), jnp.where(up, dot(mtb, zb), 0.0))
    dp = jnp.where(low, zf, jnp.where(up, zb, zf + zb))
    ds = dp * h
    n1 = da * h
    n1k = n1 * kk
    n = n1 * beta
    e = ds * (qk0 * rq * rk_r) + n1k * beta
    mt = mtf + mtb
    dbeta = dot_t(jnp.ones((16, lanes), f32), n1k + mt * yt)[0:1]
    behind = jnp.where(upto, dot(jnp.where(low, e, 0.0), up_m), 0.0)
    ahead = jnp.where(since, dot(jnp.where(up, e, 0.0), low_m), 0.0)
    ddecay = -jnp.sum(behind + ahead, axis=0, keepdims=True)
    dv = beta * dot(mt, o)
    dqn = dot(ds * rk_r, k)
    dq = rq * (dqn - qf * (rq * rq * jnp.sum(dqn * qf, axis=1, keepdims=True)))
    dkn = dot(jnp.transpose(ds * rq), q) + dot((n + jnp.transpose(n)) * rk_r, k)
    dk = rk * (dkn - kf * (rk * rk * jnp.sum(dkn * kf, axis=1, keepdims=True)))
    return (dq, dk, dv), dbeta, ddecay


class Phase:
    def __init__(self, axis, count, heads, source, gains, back, gains_back, scratch):
        self.axis, self.count, self.heads = axis, count, heads
        self.source, self.gains, self.back, self.gains_back = source, gains, back, gains_back
        (self.held, self.gains_held, self.result, self.sums, self.gains_result, self.send,
         self.recv, self.own, self.back_send, self.back_recv, self.back_own) = scratch
        self.lines = self.held.shape[1]
        self.span = self.held.shape[3]
        self.tokens = count * self.span // heads
        self.me = lax.axis_index(axis)
        self.problems = self.lines * self.tokens * heads // lanes // self.lines

    def to(self, step):
        return lax.rem(self.me + step, self.count)

    def out_copies(self, line):
        copies = []
        for step in range(self.count):
            to = self.to(step)
            if line < self.lines:
                src, dst = self.source.at[to * self.lines + line], self.held.at[self.me, line]
            else:
                src, dst = self.gains.at[to], self.gains_held.at[self.me]
            copies.append(self.copy(src, dst, step, line, to, self.send, self.recv, self.own))
        return copies

    def back_copies(self, line):
        copies = []
        for step in range(self.count):
            to = self.to(step)
            if line < self.lines:
                src, dst = self.result.at[to, line], self.back.at[self.me * self.lines + line]
            else:
                src, dst = self.gains_result, self.gains_back.at[self.me]
            copies.append(
                self.copy(src, dst, step, line, to, self.back_send, self.back_recv, self.back_own)
            )
        return copies

    def copy(self, src, dst, step, line, to, send, recv, own):
        if step == 0:
            return pltpu.make_async_copy(src, dst, own.at[line])
        return pltpu.make_async_remote_copy(
            src_ref=src,
            dst_ref=dst,
            send_sem=send.at[line, step - 1],
            recv_sem=recv.at[line, step - 1],
            device_id={self.axis: to},
            device_id_type=pl.DeviceIdType.MESH,
        )

    def solve_line(self, line, stage, grads):
        tokens, heads, span = self.tokens, self.heads, self.span
        total = tokens * heads
        for member in range(4):
            for peer in range(self.count):
                stage[pl.ds(member * total + peer * span, span), :] = self.held[
                    peer, line, member
                ].astype(f32)
        joined = lanes // tokens
        half = self.gains_held.shape[1] // 2
        gains = self.gains_held[0].astype(f32)
        for peer in range(1, self.count):
            gains = gains + self.gains_held[peer].astype(f32)
        if line == 0:
            self.sums[...] = gains

        def some(index, carry):
            for extra in range(together):
                group = index * together + extra
                row = line * self.problems + group

                def fetch(member):
                    parts = [
                        stage[pl.ds(member * total + group * joined + part, tokens, stride=heads), :]
                        for part in range(joined)
                    ]
                    return jnp.concatenate(parts, axis=0).astype(bf16)

                found, dbeta, ddecay = solve(
                    fetch(0), fetch(1), fetch(2), fetch(3),
                    self.sums[pl.ds(row, 1), :], self.sums[pl.ds(half + row, 1), :], tokens,
                )
                for member in range(3):
                    for part in range(joined):
                        place = pl.ds(member * total + group * joined + part, tokens, stride=heads)
                        grads[place, :] = found[member][part * tokens : (part + 1) * tokens]
                self.sums[pl.ds(row, 1), :] = dbeta
                self.sums[pl.ds(half + row, 1), :] = ddecay
            return carry

        lax.fori_loop(0, self.problems // together, some, 0)
        for member in range(3):
            for peer in range(self.count):
                self.result[peer, line, member] = grads[
                    pl.ds(member * total + peer * span, span), :
                ].astype(bf16)


def kernel(counts, heads, *refs):
    ins, outs, scratch = refs[:4], refs[4:8], refs[8:]
    each = (len(scratch) - 2) // 2
    stage, grads = scratch[-2:]
    row = Phase("gc", counts[0], heads, ins[0], ins[1], outs[0], outs[1], scratch[:each])
    column = Phase("gr", counts[1], heads, ins[2], ins[3], outs[2], outs[3], scratch[each:-2])

    barrier = pltpu.get_barrier_semaphore()
    for phase in (row, column):
        for step in range(1, phase.count):
            pl.semaphore_signal(
                barrier, inc=1, device_id={phase.axis: phase.to(step)},
                device_id_type=pl.DeviceIdType.MESH,
            )
    pl.semaphore_wait(barrier, row.count + column.count - 2)

    started = []

    def start(copies):
        for copy in copies[1:] + copies[:1]:
            copy.start()
        started.extend(copies[1:])
        return copies

    def arrive(copies):
        for copy in copies[1:]:
            copy.wait_recv()
        copies[0].wait()

    arriving = {}
    for phase in (row, column):
        arriving[phase.axis, phase.lines] = start(phase.out_copies(phase.lines))
    for phase in (row, column):
        for line in range(phase.lines):
            arriving[phase.axis, line] = start(phase.out_copies(line))

    returning = []
    for phase in (column, row):
        arrive(arriving[phase.axis, phase.lines])
        for line in range(phase.lines):
            arrive(arriving[phase.axis, line])
            phase.solve_line(line, stage, grads)
            returning.append(start(phase.back_copies(line)))
        phase.gains_result[...] = phase.sums[...].astype(bf16)
        returning.append(start(phase.back_copies(phase.lines)))
    for copies in returning:
        arrive(copies)
    for copy in started:
        copy.wait_send()


def spread(gains, count, own, tokens, joined):
    kinds, lines, span, heads = gains.shape
    shaped = gains.reshape(kinds, count, lines // count, span, heads // joined, joined)
    shaped = jnp.transpose(shaped, (1, 0, 2, 4, 5, 3))
    mine = (jnp.arange(count) == own)[:, None]
    placed = jnp.where(mine, shaped[..., None, :], jnp.zeros((), gains.dtype))
    return placed.reshape(count, -1, lanes)


def gather(gains, count, own, lines, span, heads, joined):
    shaped = gains.reshape(count, 2, lines // count, heads // joined, joined, count, span)
    mine = (jnp.arange(count) == own)[:, None]
    picked = jnp.sum(jnp.where(mine, shaped.astype(f32), 0.0), axis=5)
    return jnp.transpose(picked, (1, 0, 2, 5, 3, 4)).reshape(2, lines, span, heads)


def on_device(counts, queries, key_vectors, values, strength, decay_rate, out_grad):
    n_row, n_col = counts
    rows, cols, heads, size = queries.shape
    row_tokens, col_tokens = n_row * cols, n_col * rows
    row_joined, col_joined = lanes // row_tokens, lanes // col_tokens
    members = jnp.stack([queries, key_vectors, values, out_grad], axis=1)
    row_source = members.reshape(rows, 4, cols * heads, size)
    members = jnp.stack([queries, key_vectors, values, out_grad], axis=0)
    col_source = jnp.transpose(members, (2, 0, 1, 3, 4)).reshape(cols, 4, rows * heads, size)
    gains = jnp.stack([strength, decay_rate])
    row_own, col_own = lax.axis_index("gc"), lax.axis_index("gr")
    row_gains = spread(gains, n_row, row_own, row_tokens, row_joined)
    col_gains = spread(jnp.swapaxes(gains, 1, 2), n_col, col_own, col_tokens, col_joined)

    def scratch(count, lines, span, gains_rows):
        table = (gains_rows, lanes)
        sems = pltpu.SemaphoreType.DMA
        return [
            pltpu.VMEM((count, lines, 4, span, size), bf16),
            pltpu.VMEM((count,) + table, bf16),
            pltpu.VMEM((count, lines, 3, span, size), bf16),
            pltpu.VMEM(table, f32),
            pltpu.VMEM(table, bf16),
            sems((lines + 1, count - 1)),
            sems((lines + 1, count - 1)),
            sems((lines + 1,)),
            sems((lines + 1, count - 1)),
            sems((lines + 1, count - 1)),
            sems((lines + 1,)),
        ]

    most = max(row_tokens, col_tokens) * heads
    shapes = [
        jax.ShapeDtypeStruct((rows, 3, cols * heads, size), bf16),
        jax.ShapeDtypeStruct(row_gains.shape, bf16),
        jax.ShapeDtypeStruct((cols, 3, rows * heads, size), bf16),
        jax.ShapeDtypeStruct(col_gains.shape, bf16),
    ]
    row_back, row_gains_back, col_back, col_gains_back = pl.pallas_call(
        functools.partial(kernel, counts, heads),
        out_shape=shapes,
        in_specs=[pl.BlockSpec(memory_space=pl.ANY)] * 4,
        out_specs=[pl.BlockSpec(memory_space=pl.ANY)] * 4,
        scratch_shapes=scratch(n_row, rows // n_row, cols * heads, row_gains.shape[1])
        + scratch(n_col, cols // n_col, rows * heads, col_gains.shape[1])
        + [pltpu.VMEM((4 * most, size), f32), pltpu.VMEM((3 * most, size), f32)],
        compiler_params=pltpu.CompilerParams(
            collective_id=0, has_side_effects=True, vmem_limit_bytes=40 * 2**20
        ),
        name="exchange_and_solve",
    )(row_source, row_gains, col_source, col_gains)

    row_back = row_back.reshape(rows, 3, cols, heads, size)
    col_back = col_back.reshape(cols, 3, rows, heads, size)

    def merged(member):
        first = row_back[:, member].astype(f32)
        second = jnp.swapaxes(col_back[:, member], 0, 1).astype(f32)
        return (first + second).astype(bf16)

    row_small = gather(row_gains_back, n_row, row_own, rows, cols, heads, row_joined)
    col_small = gather(col_gains_back, n_col, col_own, cols, rows, heads, col_joined)
    small = (row_small + jnp.swapaxes(col_small, 1, 2)).astype(bf16)
    return (merged(0), merged(1), merged(2), small[0], small[1])


def solution(mesh):
    counts = (mesh.shape["gc"], mesh.shape["gr"])
    wide = P("gr", "gc", None, None)
    narrow = P("gr", "gc", None)
    return jax.shard_map(
        functools.partial(on_device, counts),
        mesh=mesh,
        in_specs=(wide, wide, wide, narrow, narrow, wide),
        out_specs=(wide, wide, wide, narrow, narrow),
        check_vma=False,
    )
```

```python
import functools

import jax
import jax.numpy as jnp
from jax import lax
from jax.experimental import pallas as pl
from jax.experimental.pallas import tpu as pltpu
from jax.sharding import PartitionSpec as P

bf16, f32 = jnp.bfloat16, jnp.float32
lanes = 128
together = 4


def dot(a, b):
    return lax.dot_general(
        a.astype(bf16), b.astype(bf16), (((1,), (0,)), ((), ())), preferred_element_type=f32
    )


def dot_t(a, b):
    return lax.dot_general(
        a.astype(bf16), b.astype(bf16), (((1,), (1,)), ((), ())), preferred_element_type=f32
    )


class Masks:
    def __init__(self, line):
        i = lax.broadcasted_iota(jnp.int32, (lanes, lanes), 0)
        j = lax.broadcasted_iota(jnp.int32, (lanes, lanes), 1)
        self.line, self.apart = line, i ^ j
        self.same = self.apart < line
        self.eye = self.apart == 0
        self.low, self.up = self.same & (i > j), self.same & (i < j)
        self.upto, self.since = self.same & (i >= j), self.same & (i <= j)
        names = ("low", "up", "upto", "since")
        self.ones = {
            name: jnp.where(getattr(self, name), 1.0, 0.0).astype(bf16) for name in names
        }


def unit_inverses(xs, masks):
    us = [jnp.where(masks.apart == 1, -x, 0.0) for x in xs]
    size = 2
    while size < masks.line:
        here = (masks.apart >= size) & (masks.apart < 2 * size)
        parts = [jnp.where(here, x, 0.0) for x in xs]
        lefts = [part + dot(u, part) for u, part in zip(us, parts)]
        yield
        us = [u - (left + dot(left, u)) for u, left in zip(us, lefts)]
        yield
        size *= 2
    return us


def solve(q, k, v, o, beta_r, decay_r, masks):
    eye, low, up, same = masks.eye, masks.low, masks.up, masks.same
    upto, since, ones = masks.upto, masks.since, masks.ones
    kk0, kq0 = dot_t(k, k), dot_t(k, q)
    qf, kf = q.astype(f32), k.astype(f32)
    rq = lax.rsqrt(jnp.sum(qf * qf, axis=1, keepdims=True) + 1e-6)
    rk = lax.rsqrt(jnp.sum(kf * kf, axis=1, keepdims=True) + 1e-6)
    rq_r = jnp.sum(jnp.where(eye, rq, 0.0), axis=0, keepdims=True)
    rk_r = jnp.sum(jnp.where(eye, rk, 0.0), axis=0, keepdims=True)
    gap_t = dot(jnp.where(low, decay_r, 0.0), ones["upto"])
    gap_t = gap_t + dot(jnp.where(up, decay_r, 0.0), ones["since"])
    yield
    ht = jnp.where(same, jnp.exp(-gap_t), 0.0)
    kk = kk0 * rk * rk_r
    x = kk * ht * beta_r
    uf, ub = yield from unit_inverses(
        [jnp.where(up, x, 0.0), jnp.where(low, x, 0.0)], masks
    )
    y = dot_t(o, v)
    pt = kq0 * rk * rq_r * ht
    ptf, ptb = jnp.where(low, 0.0, pt), jnp.where(up, 0.0, pt)
    mtf = ptf + dot(uf, ptf)
    mtb = ptb + dot(ub, ptb)
    yield
    yb = y * beta_r
    zf = yb + dot(yb, uf)
    zb = yb + dot(yb, ub)
    gap = dot(jnp.where(upto, decay_r, 0.0), ones["low"])
    gap = gap + dot(jnp.where(since, decay_r, 0.0), ones["up"])
    yield
    dp = jnp.where(low, zf, jnp.where(up, zb, zf + zb))
    h = jnp.where(same, jnp.exp(-gap), 0.0)
    daf, dab = dot(mtf, zf), dot(mtb, zb)
    beta = dot(jnp.where(eye, beta_r, 0.0), jnp.ones((lanes, lanes), bf16))
    qk0, yt = dot_t(q, k), dot_t(v, o)
    mt = mtf + mtb
    dv = beta * dot(mt, o)
    ds = dp * h
    dqn = dot(ds * rk_r, k)
    yield
    n1 = jnp.where(low, daf, jnp.where(up, dab, 0.0)) * -h
    n1k = n1 * kk
    n = n1 * beta
    e = ds * (qk0 * rq * rk_r) + n1k * beta
    dbeta = dot_t(jnp.ones((16, lanes), bf16), n1k + mt * yt)[0:1]
    behind = dot(jnp.where(low, e, 0.0), ones["up"])
    ahead = dot(jnp.where(up, e, 0.0), ones["low"])
    dkn = dot(jnp.transpose(ds * rq), q) + dot((n + jnp.transpose(n)) * rk_r, k)
    yield
    ddecay = jnp.where(upto, behind, 0.0) + jnp.where(since, ahead, 0.0)
    ddecay = -jnp.sum(ddecay, axis=0, keepdims=True)
    dq = rq * (dqn - qf * (rq * rq * jnp.sum(dqn * qf, axis=1, keepdims=True)))
    dk = rk * (dkn - kf * (rk * rk * jnp.sum(dkn * kf, axis=1, keepdims=True)))
    return (dq, dk, dv), dbeta, ddecay


def abreast(generators):
    results = [None] * len(generators)
    waiting = list(range(len(generators)))
    while waiting:
        for index in list(waiting):
            try:
                next(generators[index])
            except StopIteration as stop:
                results[index] = stop.value
                waiting.remove(index)
    return results


class Phase:
    def __init__(self, axis, count, heads, source, gains, back, gains_back, scratch):
        self.axis, self.count, self.heads = axis, count, heads
        self.source, self.gains, self.back, self.gains_back = source, gains, back, gains_back
        (self.held, self.gains_held, self.result, self.sums, self.gains_result, self.send,
         self.recv, self.own, self.back_send, self.back_recv, self.back_own) = scratch
        self.lines = self.held.shape[1]
        self.span = self.held.shape[3]
        self.tokens = count * self.span // heads
        self.me = lax.axis_index(axis)
        self.problems = self.lines * self.tokens * heads // lanes // self.lines

    def to(self, step):
        return lax.rem(self.me + step, self.count)

    def out_copies(self, line):
        copies = []
        for step in range(self.count):
            to = self.to(step)
            if line < self.lines:
                src, dst = self.source.at[to * self.lines + line], self.held.at[self.me, line]
            else:
                src, dst = self.gains.at[to], self.gains_held.at[self.me]
            copies.append(self.copy(src, dst, step, line, to, self.send, self.recv, self.own))
        return copies

    def back_copies(self, line):
        copies = []
        for step in range(self.count):
            to = self.to(step)
            if line < self.lines:
                src, dst = self.result.at[to, line], self.back.at[self.me * self.lines + line]
            else:
                src, dst = self.gains_result, self.gains_back.at[self.me]
            copies.append(
                self.copy(src, dst, step, line, to, self.back_send, self.back_recv, self.back_own)
            )
        return copies

    def copy(self, src, dst, step, line, to, send, recv, own):
        if step == 0:
            return pltpu.make_async_copy(src, dst, own.at[line])
        return pltpu.make_async_remote_copy(
            src_ref=src,
            dst_ref=dst,
            send_sem=send.at[line, step - 1],
            recv_sem=recv.at[line, step - 1],
            device_id={self.axis: to},
            device_id_type=pl.DeviceIdType.MESH,
        )

    def solve_line(self, line, stage, grads):
        tokens, heads, span = self.tokens, self.heads, self.span
        total = tokens * heads
        for member in range(4):
            for peer in range(self.count):
                stage[pl.ds(member * total + peer * span, span), :] = self.held[
                    peer, line, member
                ].astype(f32)
        joined = lanes // tokens
        half = self.gains_held.shape[1] // 2
        gains = self.gains_held[0].astype(f32)
        for peer in range(1, self.count):
            gains = gains + self.gains_held[peer].astype(f32)
        if line == 0:
            self.sums[...] = gains

        def fetch(group, member):
            parts = [
                stage[pl.ds(member * total + group * joined + part, tokens, stride=heads), :]
                for part in range(joined)
            ]
            return jnp.concatenate(parts, axis=0).astype(bf16)

        def some(index, carry):
            masks = Masks(tokens)
            groups = [index * together + extra for extra in range(together)]
            rows = [line * self.problems + group for group in groups]
            solving = [
                solve(
                    *(fetch(group, member) for member in range(4)),
                    self.sums[pl.ds(row, 1), :], self.sums[pl.ds(half + row, 1), :], masks,
                )
                for group, row in zip(groups, rows)
            ]
            for group, row, (found, dbeta, ddecay) in zip(groups, rows, abreast(solving)):
                for member in range(3):
                    for part in range(joined):
                        place = pl.ds(member * total + group * joined + part, tokens, stride=heads)
                        grads[place, :] = found[member][part * tokens : (part + 1) * tokens]
                self.sums[pl.ds(row, 1), :] = dbeta
                self.sums[pl.ds(half + row, 1), :] = ddecay
            return carry

        lax.fori_loop(0, self.problems // together, some, 0)
        for member in range(3):
            for peer in range(self.count):
                self.result[peer, line, member] = grads[
                    pl.ds(member * total + peer * span, span), :
                ].astype(bf16)


def kernel(counts, heads, *refs):
    ins, outs, scratch = refs[:4], refs[4:8], refs[8:]
    each = (len(scratch) - 2) // 2
    stage, grads = scratch[-2:]
    row = Phase("gc", counts[0], heads, ins[0], ins[1], outs[0], outs[1], scratch[:each])
    column = Phase("gr", counts[1], heads, ins[2], ins[3], outs[2], outs[3], scratch[each:-2])

    barrier = pltpu.get_barrier_semaphore()
    for phase in (row, column):
        for step in range(1, phase.count):
            pl.semaphore_signal(
                barrier, inc=1, device_id={phase.axis: phase.to(step)},
                device_id_type=pl.DeviceIdType.MESH,
            )
    pl.semaphore_wait(barrier, row.count + column.count - 2)

    started = []

    def start(copies):
        for copy in copies[1:] + copies[:1]:
            copy.start()
        started.extend(copies[1:])
        return copies

    def arrive(copies):
        for copy in copies[1:]:
            copy.wait_recv()
        copies[0].wait()

    arriving = {}
    for phase in (row, column):
        arriving[phase.axis, phase.lines] = start(phase.out_copies(phase.lines))
    for phase in (row, column):
        for line in range(phase.lines):
            arriving[phase.axis, line] = start(phase.out_copies(line))

    returning = []
    for phase in (column, row):
        arrive(arriving[phase.axis, phase.lines])
    for line in range(max(row.lines, column.lines)):
        for phase in (column, row):
            if line >= phase.lines:
                continue
            arrive(arriving[phase.axis, line])
            phase.solve_line(line, stage, grads)
            returning.append(start(phase.back_copies(line)))
            if line == phase.lines - 1:
                phase.gains_result[...] = phase.sums[...].astype(bf16)
                returning.append(start(phase.back_copies(phase.lines)))
    for copies in returning:
        arrive(copies)
    for copy in started:
        copy.wait_send()


def spread(gains, count, own, tokens, joined):
    kinds, lines, span, heads = gains.shape
    shaped = gains.reshape(kinds, count, lines // count, span, heads // joined, joined)
    shaped = jnp.transpose(shaped, (1, 0, 2, 4, 5, 3))
    mine = (jnp.arange(count) == own)[:, None]
    placed = jnp.where(mine, shaped[..., None, :], jnp.zeros((), gains.dtype))
    return placed.reshape(count, -1, lanes)


def gather(gains, count, own, lines, span, heads, joined):
    shaped = gains.reshape(count, 2, lines // count, heads // joined, joined, count, span)
    mine = (jnp.arange(count) == own)[:, None]
    picked = jnp.sum(jnp.where(mine, shaped.astype(f32), 0.0), axis=5)
    return jnp.transpose(picked, (1, 0, 2, 5, 3, 4)).reshape(2, lines, span, heads)


def on_device(counts, queries, key_vectors, values, strength, decay_rate, out_grad):
    n_row, n_col = counts
    rows, cols, heads, size = queries.shape
    row_tokens, col_tokens = n_row * cols, n_col * rows
    row_joined, col_joined = lanes // row_tokens, lanes // col_tokens
    members = jnp.stack([queries, key_vectors, values, out_grad], axis=1)
    row_source = members.reshape(rows, 4, cols * heads, size)
    members = jnp.stack([queries, key_vectors, values, out_grad], axis=0)
    col_source = jnp.transpose(members, (2, 0, 1, 3, 4)).reshape(cols, 4, rows * heads, size)
    gains = jnp.stack([strength, decay_rate])
    row_own, col_own = lax.axis_index("gc"), lax.axis_index("gr")
    row_gains = spread(gains, n_row, row_own, row_tokens, row_joined)
    col_gains = spread(jnp.swapaxes(gains, 1, 2), n_col, col_own, col_tokens, col_joined)

    def scratch(count, lines, span, gains_rows):
        table = (gains_rows, lanes)
        sems = pltpu.SemaphoreType.DMA
        return [
            pltpu.VMEM((count, lines, 4, span, size), bf16),
            pltpu.VMEM((count,) + table, bf16),
            pltpu.VMEM((count, lines, 3, span, size), bf16),
            pltpu.VMEM(table, f32),
            pltpu.VMEM(table, bf16),
            sems((lines + 1, count - 1)),
            sems((lines + 1, count - 1)),
            sems((lines + 1,)),
            sems((lines + 1, count - 1)),
            sems((lines + 1, count - 1)),
            sems((lines + 1,)),
        ]

    most = max(row_tokens, col_tokens) * heads
    shapes = [
        jax.ShapeDtypeStruct((rows, 3, cols * heads, size), bf16),
        jax.ShapeDtypeStruct(row_gains.shape, bf16),
        jax.ShapeDtypeStruct((cols, 3, rows * heads, size), bf16),
        jax.ShapeDtypeStruct(col_gains.shape, bf16),
    ]
    row_back, row_gains_back, col_back, col_gains_back = pl.pallas_call(
        functools.partial(kernel, counts, heads),
        out_shape=shapes,
        in_specs=[pl.BlockSpec(memory_space=pl.ANY)] * 4,
        out_specs=[pl.BlockSpec(memory_space=pl.ANY)] * 4,
        scratch_shapes=scratch(n_row, rows // n_row, cols * heads, row_gains.shape[1])
        + scratch(n_col, cols // n_col, rows * heads, col_gains.shape[1])
        + [pltpu.VMEM((4 * most, size), f32), pltpu.VMEM((3 * most, size), f32)],
        compiler_params=pltpu.CompilerParams(
            collective_id=0, has_side_effects=True, vmem_limit_bytes=40 * 2**20
        ),
        name="exchange_and_solve",
    )(row_source, row_gains, col_source, col_gains)

    row_back = row_back.reshape(rows, 3, cols, heads, size)
    col_back = col_back.reshape(cols, 3, rows, heads, size)

    def merged(member):
        first = row_back[:, member].astype(f32)
        second = jnp.swapaxes(col_back[:, member], 0, 1).astype(f32)
        return (first + second).astype(bf16)

    row_small = gather(row_gains_back, n_row, row_own, rows, cols, heads, row_joined)
    col_small = gather(col_gains_back, n_col, col_own, cols, rows, heads, col_joined)
    small = (row_small + jnp.swapaxes(col_small, 1, 2)).astype(bf16)
    return (merged(0), merged(1), merged(2), small[0], small[1])


def solution(mesh):
    counts = (mesh.shape["gc"], mesh.shape["gr"])
    wide = P("gr", "gc", None, None)
    narrow = P("gr", "gc", None)
    return jax.shard_map(
        functools.partial(on_device, counts),
        mesh=mesh,
        in_specs=(wide, wide, wide, narrow, narrow, wide),
        out_specs=(wide, wide, wide, narrow, narrow),
        check_vma=False,
    )
```

```python
import functools

import jax
import jax.numpy as jnp
from jax import lax
from jax.experimental import pallas as pl
from jax.experimental.pallas import tpu as pltpu
from jax.sharding import PartitionSpec as P

bf16, f32 = jnp.bfloat16, jnp.float32
lanes = 128
together = 4


def dot(a, b):
    return lax.dot_general(
        a.astype(bf16), b.astype(bf16), (((1,), (0,)), ((), ())), preferred_element_type=f32
    )


def dot_t(a, b):
    return lax.dot_general(
        a.astype(bf16), b.astype(bf16), (((1,), (1,)), ((), ())), preferred_element_type=f32
    )


class Masks:
    def __init__(self, line):
        i = lax.broadcasted_iota(jnp.int32, (lanes, lanes), 0)
        j = lax.broadcasted_iota(jnp.int32, (lanes, lanes), 1)
        self.line, self.apart = line, i ^ j
        self.same = self.apart < line
        self.eye = self.apart == 0
        self.low, self.up = self.same & (i > j), self.same & (i < j)
        self.upto, self.since = self.same & (i >= j), self.same & (i <= j)
        names = ("low", "up", "upto", "since")
        self.ones = {
            name: jnp.where(getattr(self, name), 1.0, 0.0).astype(bf16) for name in names
        }


def unit_inverses(xs, masks):
    us = [jnp.where(masks.apart == 1, -x, 0.0) for x in xs]
    size = 2
    while size < masks.line:
        here = (masks.apart >= size) & (masks.apart < 2 * size)
        parts = [jnp.where(here, x, 0.0) for x in xs]
        lefts = [part + dot(u, part) for u, part in zip(us, parts)]
        yield
        us = [u - (left + dot(left, u)) for u, left in zip(us, lefts)]
        yield
        size *= 2
    return us


def solve(q, k, v, o, beta_r, decay_r, masks):
    eye, low, up, same = masks.eye, masks.low, masks.up, masks.same
    upto, since, ones = masks.upto, masks.since, masks.ones
    kk0, kq0 = dot_t(k, k), dot_t(k, q)
    qf, kf = q.astype(f32), k.astype(f32)
    rq = lax.rsqrt(jnp.sum(qf * qf, axis=1, keepdims=True) + 1e-6)
    rk = lax.rsqrt(jnp.sum(kf * kf, axis=1, keepdims=True) + 1e-6)
    rq_r = jnp.sum(jnp.where(eye, rq, 0.0), axis=0, keepdims=True)
    rk_r = jnp.sum(jnp.where(eye, rk, 0.0), axis=0, keepdims=True)
    gap_t = dot(jnp.where(low, decay_r, 0.0), ones["upto"])
    gap_t = gap_t + dot(jnp.where(up, decay_r, 0.0), ones["since"])
    yield
    ht = jnp.where(same, jnp.exp(-gap_t), 0.0)
    kk = kk0 * rk * rk_r
    x = kk * ht * beta_r
    uf, ub = yield from unit_inverses(
        [jnp.where(up, x, 0.0), jnp.where(low, x, 0.0)], masks
    )
    y = dot_t(o, v)
    pt = kq0 * rk * rq_r * ht
    ptf, ptb = jnp.where(low, 0.0, pt), jnp.where(up, 0.0, pt)
    mtf = ptf + dot(uf, ptf)
    mtb = ptb + dot(ub, ptb)
    yield
    yb = y * beta_r
    zf = yb + dot(yb, uf)
    zb = yb + dot(yb, ub)
    gap = dot(jnp.where(upto, decay_r, 0.0), ones["low"])
    gap = gap + dot(jnp.where(since, decay_r, 0.0), ones["up"])
    yield
    dp = jnp.where(low, zf, jnp.where(up, zb, zf + zb))
    h = jnp.where(same, jnp.exp(-gap), 0.0)
    daf, dab = dot(mtf, zf), dot(mtb, zb)
    beta = dot(jnp.where(eye, beta_r, 0.0), jnp.ones((lanes, lanes), bf16))
    qk0, yt = dot_t(q, k), dot_t(v, o)
    mt = mtf + mtb
    dv = beta * dot(mt, o)
    ds = dp * h
    dqn = dot(ds * rk_r, k)
    yield
    n1 = jnp.where(low, daf, jnp.where(up, dab, 0.0)) * -h
    n1k = n1 * kk
    n = n1 * beta
    e = ds * (qk0 * rq * rk_r) + n1k * beta
    dbeta = dot_t(jnp.ones((16, lanes), bf16), n1k + mt * yt)[0:1]
    behind = dot(jnp.where(low, e, 0.0), ones["up"])
    ahead = dot(jnp.where(up, e, 0.0), ones["low"])
    dkn = dot(jnp.transpose(ds * rq), q) + dot((n + jnp.transpose(n)) * rk_r, k)
    yield
    ddecay = jnp.where(upto, behind, 0.0) + jnp.where(since, ahead, 0.0)
    ddecay = -jnp.sum(ddecay, axis=0, keepdims=True)
    dq = rq * (dqn - qf * (rq * rq * jnp.sum(dqn * qf, axis=1, keepdims=True)))
    dk = rk * (dkn - kf * (rk * rk * jnp.sum(dkn * kf, axis=1, keepdims=True)))
    return (dq, dk, dv), dbeta, ddecay


def abreast(generators):
    results = [None] * len(generators)
    waiting = list(range(len(generators)))
    while waiting:
        for index in list(waiting):
            try:
                next(generators[index])
            except StopIteration as stop:
                results[index] = stop.value
                waiting.remove(index)
    return results


class Phase:
    def __init__(self, axis, count, heads, source, back, scratch):
        self.axis, self.count, self.heads = axis, count, heads
        self.source, self.back = source, back
        (self.held, self.gains, self.gains_held, self.gains_result, self.gains_back, self.result,
         self.sums, self.send, self.recv, self.own, self.back_send, self.back_recv,
         self.back_own) = scratch
        self.lines = self.held.shape[1]
        self.span = self.held.shape[3]
        self.tokens = count * self.span // heads
        self.me = lax.axis_index(axis)
        self.problems = self.lines * self.tokens * heads // lanes // self.lines

        self.joined = lanes // self.tokens

    def placing(self, peer):
        own = lax.broadcasted_iota(jnp.int32, (lanes, lanes), 0)
        lane = lax.broadcasted_iota(jnp.int32, (lanes, lanes), 1)
        token = peer * (self.span // self.heads) + own // self.heads
        fits = (lane % self.tokens == token) & (lane // self.tokens == own % self.joined)
        return jnp.where(fits, 1.0, 0.0).astype(bf16)

    def row_masks(self):
        table, held = self.sums.shape[0], self.gains_held.shape[1]
        row = lax.broadcasted_iota(jnp.int32, (table, held), 0)
        member = lax.broadcasted_iota(jnp.int32, (table, held), 1)
        reads = jnp.where(row // self.problems == member, 1.0, 0.0).astype(bf16)
        row = lax.broadcasted_iota(jnp.int32, (table, lanes), 0)
        lane = lax.broadcasted_iota(jnp.int32, (table, lanes), 1)
        return reads, lane % self.heads // self.joined == row % self.problems

    def owner_maps(self, cells):
        columns = self.lines * self.count if self.axis == "gr" else self.span // self.heads

        def line_of(token):
            return token % columns if self.axis == "gr" else token // columns

        def place_of(token):
            return token // columns if self.axis == "gr" else token % columns

        token = lax.broadcasted_iota(jnp.int32, (cells, lanes), 0)
        lane = lax.broadcasted_iota(jnp.int32, (cells, lanes), 1)
        fits = place_of(token) == lane // self.heads
        head = lax.broadcasted_iota(jnp.int32, (self.heads, lanes), 0)
        lane = lax.broadcasted_iota(jnp.int32, (self.heads, lanes), 1)
        repeat = jnp.where(lane % self.heads == head, 1.0, 0.0).astype(bf16)
        depth = self.gains.shape[1]
        shape = (self.count * depth, cells)
        row = lax.broadcasted_iota(jnp.int32, shape, 0)
        line = line_of(lax.broadcasted_iota(jnp.int32, shape, 1))
        held = (line // self.lines == row // depth) & (line % self.lines == row % depth // 2)
        rows = [
            jnp.where(held & (row % 2 == kind), 1.0, 0.0).astype(bf16) for kind in range(2)
        ]
        return fits, repeat, rows

    def offer_gains(self, kinds):
        fits, repeat, rows = self.owner_maps(kinds[0].shape[0])
        wide = [jnp.where(fits, dot(kind[...], repeat), 0.0) for kind in kinds]
        packed = dot(rows[0], wide[0]) + dot(rows[1], wide[1])
        self.gains[...] = packed.astype(bf16).reshape(self.gains.shape)

    def collect_gains(self, cells):
        fits, repeat, rows = self.owner_maps(cells)
        packed = self.gains_back[...].reshape(-1, lanes)
        wide = [
            lax.dot_general(member, packed, (((0,), (0,)), ((), ())), preferred_element_type=f32)
            for member in rows
        ]
        return [dot_t(jnp.where(fits, member, 0.0), repeat) for member in wide]

    def unpack_gains(self):
        reads, holds = self.row_masks()
        table = jnp.zeros(self.sums.shape, f32)
        for peer in range(self.count):
            rows = jnp.where(holds, dot(reads, self.gains_held[peer]), 0.0)
            table = table + dot(rows, self.placing(peer))
        self.sums[...] = table

    def pack_gains(self):
        reads, holds = self.row_masks()
        table = self.sums[...].astype(bf16)
        for peer in range(self.count):
            rows = jnp.where(holds, dot_t(table, self.placing(peer)), 0.0).astype(bf16)
            packed = lax.dot_general(
                reads, rows, (((0,), (0,)), ((), ())), preferred_element_type=f32
            )
            self.gains_result[peer] = packed.astype(bf16)

    def to(self, step):
        return lax.rem(self.me + step, self.count)

    def out_copies(self, line):
        copies = []
        for step in range(self.count):
            to = self.to(step)
            if line < self.lines:
                src, dst = self.source.at[to * self.lines + line], self.held.at[self.me, line]
            else:
                src, dst = self.gains.at[to], self.gains_held.at[self.me]
            copies.append(self.copy(src, dst, step, line, to, self.send, self.recv, self.own))
        return copies

    def back_copies(self, line):
        copies = []
        for step in range(self.count):
            to = self.to(step)
            if line < self.lines:
                src, dst = self.result.at[to, line], self.back.at[self.me * self.lines + line]
            else:
                src, dst = self.gains_result.at[to], self.gains_back.at[self.me]
            copies.append(
                self.copy(src, dst, step, line, to, self.back_send, self.back_recv, self.back_own)
            )
        return copies

    def copy(self, src, dst, step, line, to, send, recv, own):
        if step == 0:
            return pltpu.make_async_copy(src, dst, own.at[line])
        return pltpu.make_async_remote_copy(
            src_ref=src,
            dst_ref=dst,
            send_sem=send.at[line, step - 1],
            recv_sem=recv.at[line, step - 1],
            device_id={self.axis: to},
            device_id_type=pl.DeviceIdType.MESH,
        )

    def solve_line(self, line, stage, grads):
        tokens, heads, span = self.tokens, self.heads, self.span
        total = tokens * heads
        for member in range(4):
            for peer in range(self.count):
                stage[pl.ds(member * total + peer * span, span), :] = self.held[
                    peer, line, member
                ].astype(f32)
        joined = self.joined
        first = 2 * line * self.problems

        def fetch(group, member):
            parts = [
                stage[pl.ds(member * total + group * joined + part, tokens, stride=heads), :]
                for part in range(joined)
            ]
            return jnp.concatenate(parts, axis=0).astype(bf16)

        def some(index, carry):
            masks = Masks(tokens)
            groups = [index * together + extra for extra in range(together)]
            rows = [first + group for group in groups]
            solving = [
                solve(
                    *(fetch(group, member) for member in range(4)),
                    self.sums[pl.ds(row, 1), :], self.sums[pl.ds(self.problems + row, 1), :], masks,
                )
                for group, row in zip(groups, rows)
            ]
            for group, row, (found, dbeta, ddecay) in zip(groups, rows, abreast(solving)):
                for member in range(3):
                    for part in range(joined):
                        place = pl.ds(member * total + group * joined + part, tokens, stride=heads)
                        grads[place, :] = found[member][part * tokens : (part + 1) * tokens]
                self.sums[pl.ds(row, 1), :] = dbeta
                self.sums[pl.ds(self.problems + row, 1), :] = ddecay
            return carry

        lax.fori_loop(0, self.problems // together, some, 0)
        for member in range(3):
            for peer in range(self.count):
                self.result[peer, line, member] = grads[
                    pl.ds(member * total + peer * span, span), :
                ].astype(bf16)


def kernel(counts, heads, *refs):
    ins, outs, scratch = refs[:4], refs[4:8], refs[8:]
    each = (len(scratch) - 2) // 2
    stage, grads = scratch[-2:]
    row = Phase("gc", counts[0], heads, ins[0], outs[0], scratch[:each])
    column = Phase("gr", counts[1], heads, ins[1], outs[1], scratch[each:-2])

    barrier = pltpu.get_barrier_semaphore()
    for phase in (row, column):
        for step in range(1, phase.count):
            pl.semaphore_signal(
                barrier, inc=1, device_id={phase.axis: phase.to(step)},
                device_id_type=pl.DeviceIdType.MESH,
            )
    pl.semaphore_wait(barrier, row.count + column.count - 2)

    started = []

    def start(copies):
        for copy in copies[1:] + copies[:1]:
            copy.start()
        started.extend(copies[1:])
        return copies

    def arrive(copies):
        for copy in copies[1:]:
            copy.wait_recv()
        copies[0].wait()

    arriving = {}
    for phase in (row, column):
        for line in range(phase.lines):
            arriving[phase.axis, line] = start(phase.out_copies(line))
            if line == 0:
                phase.offer_gains(ins[2:])
                arriving[phase.axis, phase.lines] = start(phase.out_copies(phase.lines))

    returning, gains_returning = [], []
    for line in range(max(row.lines, column.lines)):
        for phase in (column, row):
            if line >= phase.lines:
                continue
            arrive(arriving[phase.axis, line])
            if line == 0:
                arrive(arriving[phase.axis, phase.lines])
                phase.unpack_gains()
            phase.solve_line(line, stage, grads)
            if line == phase.lines - 1:
                phase.pack_gains()
                gains_returning.append(start(phase.back_copies(phase.lines)))
            returning.append(start(phase.back_copies(line)))
    for copies in gains_returning:
        arrive(copies)
    found = [phase.collect_gains(ins[2].shape[0]) for phase in (row, column)]
    for kind in range(2):
        rounded = [member[kind].astype(bf16).astype(f32) for member in found]
        outs[2 + kind][...] = (rounded[0] + rounded[1]).astype(bf16)
    for copies in returning:
        arrive(copies)
    for copy in started:
        copy.wait_send()


def on_device(counts, queries, key_vectors, values, strength, decay_rate, out_grad):
    n_row, n_col = counts
    rows, cols, heads, size = queries.shape
    row_tokens, col_tokens = n_row * cols, n_col * rows
    members = jnp.stack([queries, key_vectors, values, out_grad], axis=1)
    row_source = members.reshape(rows, 4, cols * heads, size)
    members = jnp.stack([queries, key_vectors, values, out_grad], axis=0)
    col_source = jnp.transpose(members, (2, 0, 1, 3, 4)).reshape(cols, 4, rows * heads, size)

    def scratch(count, lines, span):
        held = (count, 2 * lines + -2 * lines % 16, lanes)
        table = (2 * lines * count * span // lanes, lanes)
        sems = pltpu.SemaphoreType.DMA
        return [
            pltpu.VMEM((count, lines, 4, span, size), bf16),
            pltpu.VMEM(held, bf16),
            pltpu.VMEM(held, bf16),
            pltpu.VMEM(held, bf16),
            pltpu.VMEM(held, bf16),
            pltpu.VMEM((count, lines, 3, span, size), bf16),
            pltpu.VMEM(table, f32),
            sems((lines + 1, count - 1)),
            sems((lines + 1, count - 1)),
            sems((lines + 1,)),
            sems((lines + 1, count - 1)),
            sems((lines + 1, count - 1)),
            sems((lines + 1,)),
        ]

    most = max(row_tokens, col_tokens) * heads
    shapes = [
        jax.ShapeDtypeStruct((rows, 3, cols * heads, size), bf16),
        jax.ShapeDtypeStruct((cols, 3, rows * heads, size), bf16),
        jax.ShapeDtypeStruct((rows * cols, heads), bf16),
        jax.ShapeDtypeStruct((rows * cols, heads), bf16),
    ]
    places = [pl.BlockSpec(memory_space=pl.ANY)] * 2 + [pl.BlockSpec(memory_space=pltpu.VMEM)] * 2
    row_back, col_back, strength_grad, decay_grad = pl.pallas_call(
        functools.partial(kernel, counts, heads),
        out_shape=shapes,
        in_specs=places,
        out_specs=places,
        scratch_shapes=scratch(n_row, rows // n_row, cols * heads)
        + scratch(n_col, cols // n_col, rows * heads)
        + [pltpu.VMEM((4 * most, size), f32), pltpu.VMEM((3 * most, size), f32)],
        compiler_params=pltpu.CompilerParams(
            collective_id=0, has_side_effects=True, vmem_limit_bytes=40 * 2**20
        ),
        name="exchange_and_solve",
    )(
        row_source,
        col_source,
        strength.reshape(rows * cols, heads),
        decay_rate.reshape(rows * cols, heads),
    )

    row_back = row_back.reshape(rows, 3, cols, heads, size)
    col_back = col_back.reshape(cols, 3, rows, heads, size)

    def merged(member):
        first = row_back[:, member].astype(f32)
        second = jnp.swapaxes(col_back[:, member], 0, 1).astype(f32)
        return (first + second).astype(bf16)

    small = [member.reshape(rows, cols, heads) for member in (strength_grad, decay_grad)]
    return (merged(0), merged(1), merged(2), small[0], small[1])


def solution(mesh):
    counts = (mesh.shape["gc"], mesh.shape["gr"])
    wide = P("gr", "gc", None, None)
    narrow = P("gr", "gc", None)
    return jax.shard_map(
        functools.partial(on_device, counts),
        mesh=mesh,
        in_specs=(wide, wide, wide, narrow, narrow, wide),
        out_specs=(wide, wide, wide, narrow, narrow),
        check_vma=False,
    )
```

```python
import functools

import jax
import jax.numpy as jnp
from jax import lax
from jax.experimental import pallas as pl
from jax.experimental.pallas import tpu as pltpu
from jax.sharding import PartitionSpec as P

bf16, f32 = jnp.bfloat16, jnp.float32
lanes = 128
together = 4


def dot(a, b):
    return lax.dot_general(
        a.astype(bf16), b.astype(bf16), (((1,), (0,)), ((), ())), preferred_element_type=f32
    )


def dot_t(a, b):
    return lax.dot_general(
        a.astype(bf16), b.astype(bf16), (((1,), (1,)), ((), ())), preferred_element_type=f32
    )


class Masks:
    def __init__(self, line):
        i = lax.broadcasted_iota(jnp.int32, (lanes, lanes), 0)
        j = lax.broadcasted_iota(jnp.int32, (lanes, lanes), 1)
        self.line, self.apart = line, i ^ j
        self.same = self.apart < line
        self.eye = self.apart == 0
        self.low, self.up = self.same & (i > j), self.same & (i < j)
        self.upto, self.since = self.same & (i >= j), self.same & (i <= j)
        names = ("low", "up", "upto", "since")
        self.ones = {
            name: jnp.where(getattr(self, name), 1.0, 0.0).astype(bf16) for name in names
        }


def unit_inverses(xs, masks):
    us = [jnp.where(masks.apart == 1, -x, 0.0) for x in xs]
    size = 2
    while size < masks.line:
        here = (masks.apart >= size) & (masks.apart < 2 * size)
        parts = [jnp.where(here, x, 0.0) for x in xs]
        lefts = [part + dot(u, part) for u, part in zip(us, parts)]
        yield
        us = [u - (left + dot(left, u)) for u, left in zip(us, lefts)]
        yield
        size *= 2
    return us


def solve(q, k, v, o, beta_r, decay_r, masks):
    eye, low, up, same = masks.eye, masks.low, masks.up, masks.same
    upto, since, ones = masks.upto, masks.since, masks.ones
    kk0, kq0 = dot_t(k, k), dot_t(k, q)
    qf, kf = q.astype(f32), k.astype(f32)
    rq = lax.rsqrt(jnp.sum(qf * qf, axis=1, keepdims=True) + 1e-6)
    rk = lax.rsqrt(jnp.sum(kf * kf, axis=1, keepdims=True) + 1e-6)
    rq_r = jnp.sum(jnp.where(eye, rq, 0.0), axis=0, keepdims=True)
    rk_r = jnp.sum(jnp.where(eye, rk, 0.0), axis=0, keepdims=True)
    gap_t = dot(jnp.where(low, decay_r, 0.0), ones["upto"])
    gap_t = gap_t + dot(jnp.where(up, decay_r, 0.0), ones["since"])
    yield
    ht = jnp.where(same, jnp.exp(-gap_t), 0.0)
    kk = kk0 * rk * rk_r
    x = kk * ht * beta_r
    uf, ub = yield from unit_inverses(
        [jnp.where(up, x, 0.0), jnp.where(low, x, 0.0)], masks
    )
    y = dot_t(o, v)
    pt = kq0 * rk * rq_r * ht
    ptf, ptb = jnp.where(low, 0.0, pt), jnp.where(up, 0.0, pt)
    mtf = ptf + dot(uf, ptf)
    mtb = ptb + dot(ub, ptb)
    yield
    yb = y * beta_r
    zf = yb + dot(yb, uf)
    zb = yb + dot(yb, ub)
    gap = dot(jnp.where(upto, decay_r, 0.0), ones["low"])
    gap = gap + dot(jnp.where(since, decay_r, 0.0), ones["up"])
    yield
    dp = jnp.where(low, zf, jnp.where(up, zb, zf + zb))
    h = jnp.where(same, jnp.exp(-gap), 0.0)
    daf, dab = dot(mtf, zf), dot(mtb, zb)
    beta = dot(jnp.where(eye, beta_r, 0.0), jnp.ones((lanes, lanes), bf16))
    qk0, yt = dot_t(q, k), dot_t(v, o)
    mt = mtf + mtb
    dv = beta * dot(mt, o)
    ds = dp * h
    dqn = dot(ds * rk_r, k)
    yield
    n1 = jnp.where(low, daf, jnp.where(up, dab, 0.0)) * -h
    n1k = n1 * kk
    n = n1 * beta
    e = ds * (qk0 * rq * rk_r) + n1k * beta
    dbeta = dot_t(jnp.ones((16, lanes), bf16), n1k + mt * yt)[0:1]
    behind = dot(jnp.where(low, e, 0.0), ones["up"])
    ahead = dot(jnp.where(up, e, 0.0), ones["low"])
    dkn = dot(jnp.transpose(ds * rq), q) + dot((n + jnp.transpose(n)) * rk_r, k)
    yield
    ddecay = jnp.where(upto, behind, 0.0) + jnp.where(since, ahead, 0.0)
    ddecay = -jnp.sum(ddecay, axis=0, keepdims=True)
    dq = rq * (dqn - qf * (rq * rq * jnp.sum(dqn * qf, axis=1, keepdims=True)))
    dk = rk * (dkn - kf * (rk * rk * jnp.sum(dkn * kf, axis=1, keepdims=True)))
    return (dq, dk, dv), dbeta, ddecay


def abreast(generators):
    results = [None] * len(generators)
    waiting = list(range(len(generators)))
    while waiting:
        for index in list(waiting):
            try:
                next(generators[index])
            except StopIteration as stop:
                results[index] = stop.value
                waiting.remove(index)
    return results


class Phase:
    def __init__(self, axis, count, heads, source, back, scratch):
        self.axis, self.count, self.heads = axis, count, heads
        self.source, self.back = source, back
        (self.held, self.gains, self.gains_held, self.gains_result, self.gains_back, self.result,
         self.sums, self.send, self.recv, self.own, self.back_send, self.back_recv,
         self.back_own) = scratch
        self.lines = self.held.shape[1]
        self.span = self.held.shape[3]
        self.tokens = count * self.span // heads
        self.me = lax.axis_index(axis)
        self.problems = self.lines * self.tokens * heads // lanes // self.lines

        self.joined = lanes // self.tokens

    def placing(self, peer):
        own = lax.broadcasted_iota(jnp.int32, (lanes, lanes), 0)
        lane = lax.broadcasted_iota(jnp.int32, (lanes, lanes), 1)
        token = peer * (self.span // self.heads) + own // self.heads
        fits = (lane % self.tokens == token) & (lane // self.tokens == own % self.joined)
        return jnp.where(fits, 1.0, 0.0).astype(bf16)

    def row_masks(self):
        table, held = self.sums.shape[0], self.gains_held.shape[1]
        row = lax.broadcasted_iota(jnp.int32, (table, held), 0)
        member = lax.broadcasted_iota(jnp.int32, (table, held), 1)
        reads = jnp.where(row // self.problems == member, 1.0, 0.0).astype(bf16)
        row = lax.broadcasted_iota(jnp.int32, (table, lanes), 0)
        lane = lax.broadcasted_iota(jnp.int32, (table, lanes), 1)
        return reads, lane % self.heads // self.joined == row % self.problems

    def owner_maps(self, cells):
        columns = self.lines * self.count if self.axis == "gr" else self.span // self.heads

        def line_of(token):
            return token % columns if self.axis == "gr" else token // columns

        def place_of(token):
            return token // columns if self.axis == "gr" else token % columns

        token = lax.broadcasted_iota(jnp.int32, (cells, lanes), 0)
        lane = lax.broadcasted_iota(jnp.int32, (cells, lanes), 1)
        fits = place_of(token) == lane // self.heads
        head = lax.broadcasted_iota(jnp.int32, (self.heads, lanes), 0)
        lane = lax.broadcasted_iota(jnp.int32, (self.heads, lanes), 1)
        repeat = jnp.where(lane % self.heads == head, 1.0, 0.0).astype(bf16)
        depth = self.gains.shape[1]
        shape = (self.count * depth, cells)
        row = lax.broadcasted_iota(jnp.int32, shape, 0)
        line = line_of(lax.broadcasted_iota(jnp.int32, shape, 1))
        held = (line // self.lines == row // depth) & (line % self.lines == row % depth // 2)
        rows = [
            jnp.where(held & (row % 2 == kind), 1.0, 0.0).astype(bf16) for kind in range(2)
        ]
        return fits, repeat, rows

    def offer_gains(self, kinds):
        fits, repeat, rows = self.owner_maps(kinds[0].shape[0])
        wide = [jnp.where(fits, dot(kind, repeat), 0.0) for kind in kinds]
        packed = dot(rows[0], wide[0]) + dot(rows[1], wide[1])
        self.gains[...] = packed.astype(bf16).reshape(self.gains.shape)

    def collect_gains(self, cells):
        fits, repeat, rows = self.owner_maps(cells)
        packed = self.gains_back[...].reshape(-1, lanes)
        wide = [
            lax.dot_general(member, packed, (((0,), (0,)), ((), ())), preferred_element_type=f32)
            for member in rows
        ]
        return [dot_t(jnp.where(fits, member, 0.0), repeat) for member in wide]

    def unpack_gains(self):
        reads, holds = self.row_masks()
        table = jnp.zeros(self.sums.shape, f32)
        for peer in range(self.count):
            rows = jnp.where(holds, dot(reads, self.gains_held[peer]), 0.0)
            table = table + dot(rows, self.placing(peer))
        self.sums[...] = table

    def pack_gains(self):
        reads, holds = self.row_masks()
        table = self.sums[...].astype(bf16)
        for peer in range(self.count):
            rows = jnp.where(holds, dot_t(table, self.placing(peer)), 0.0).astype(bf16)
            packed = lax.dot_general(
                reads, rows, (((0,), (0,)), ((), ())), preferred_element_type=f32
            )
            self.gains_result[peer] = packed.astype(bf16)

    def to(self, step):
        return lax.rem(self.me + step, self.count)

    def out_copies(self, line):
        copies = []
        for step in range(self.count):
            to = self.to(step)
            if line < self.lines:
                src, dst = self.source.at[to * self.lines + line], self.held.at[self.me, line]
            else:
                src, dst = self.gains.at[to], self.gains_held.at[self.me]
            copies.append(self.copy(src, dst, step, line, to, self.send, self.recv, self.own))
        return copies

    def back_copies(self, line):
        copies = []
        for step in range(self.count):
            to = self.to(step)
            if line < self.lines:
                src, dst = self.result.at[to, line], self.back.at[self.me * self.lines + line]
            else:
                src, dst = self.gains_result.at[to], self.gains_back.at[self.me]
            copies.append(
                self.copy(src, dst, step, line, to, self.back_send, self.back_recv, self.back_own)
            )
        return copies

    def copy(self, src, dst, step, line, to, send, recv, own):
        if step == 0:
            return pltpu.make_async_copy(src, dst, own.at[line])
        return pltpu.make_async_remote_copy(
            src_ref=src,
            dst_ref=dst,
            send_sem=send.at[line, step - 1],
            recv_sem=recv.at[line, step - 1],
            device_id={self.axis: to},
            device_id_type=pl.DeviceIdType.MESH,
        )

    def solve_line(self, line, stage, grads):
        tokens, heads, span = self.tokens, self.heads, self.span
        total = tokens * heads
        for member in range(4):
            for peer in range(self.count):
                stage[pl.ds(member * total + peer * span, span), :] = self.held[
                    peer, line, member
                ].astype(f32)
        joined = self.joined
        first = 2 * line * self.problems

        def fetch(group, member):
            parts = [
                stage[pl.ds(member * total + group * joined + part, tokens, stride=heads), :]
                for part in range(joined)
            ]
            return jnp.concatenate(parts, axis=0).astype(bf16)

        def some(index, carry):
            masks = Masks(tokens)
            groups = [index * together + extra for extra in range(together)]
            rows = [first + group for group in groups]
            solving = [
                solve(
                    *(fetch(group, member) for member in range(4)),
                    self.sums[pl.ds(row, 1), :], self.sums[pl.ds(self.problems + row, 1), :], masks,
                )
                for group, row in zip(groups, rows)
            ]
            for group, row, (found, dbeta, ddecay) in zip(groups, rows, abreast(solving)):
                for member in range(3):
                    for part in range(joined):
                        place = pl.ds(member * total + group * joined + part, tokens, stride=heads)
                        grads[place, :] = found[member][part * tokens : (part + 1) * tokens]
                self.sums[pl.ds(row, 1), :] = dbeta
                self.sums[pl.ds(self.problems + row, 1), :] = ddecay
            return carry

        lax.fori_loop(0, self.problems // together, some, 0)
        for member in range(3):
            for peer in range(self.count):
                self.result[peer, line, member] = grads[
                    pl.ds(member * total + peer * span, span), :
                ].astype(bf16)


def kernel(counts, heads, *refs):
    ins, outs, scratch = refs[:4], refs[4:8], refs[8:]
    each = (len(scratch) - 2) // 2
    stage, grads = scratch[-2:]
    row = Phase("gc", counts[0], heads, ins[0], outs[0], scratch[:each])
    column = Phase("gr", counts[1], heads, ins[1], outs[1], scratch[each:-2])

    barrier = pltpu.get_barrier_semaphore()
    for phase in (row, column):
        for step in range(1, phase.count):
            pl.semaphore_signal(
                barrier, inc=1, device_id={phase.axis: phase.to(step)},
                device_id_type=pl.DeviceIdType.MESH,
            )
    pl.semaphore_wait(barrier, row.count + column.count - 2)

    started = []

    def start(copies):
        for copy in copies[1:] + copies[:1]:
            copy.start()
        started.extend(copies[1:])
        return copies

    def arrive(copies):
        for copy in copies[1:]:
            copy.wait_recv()
        copies[0].wait()

    arriving = {}
    for phase in (row, column):
        for line in range(phase.lines):
            arriving[phase.axis, line] = start(phase.out_copies(line))
            if line == 0:
                phase.offer_gains([kind[...].astype(f32).reshape(-1, heads) for kind in ins[2:]])
                arriving[phase.axis, phase.lines] = start(phase.out_copies(phase.lines))

    returning, gains_returning = [], []
    for line in range(max(row.lines, column.lines)):
        for phase in (column, row):
            if line >= phase.lines:
                continue
            arrive(arriving[phase.axis, line])
            if line == 0:
                arrive(arriving[phase.axis, phase.lines])
                phase.unpack_gains()
            phase.solve_line(line, stage, grads)
            if line == phase.lines - 1:
                phase.pack_gains()
                gains_returning.append(start(phase.back_copies(phase.lines)))
            returning.append(start(phase.back_copies(line)))
    for copies in gains_returning:
        arrive(copies)
    cells = ins[2].shape[0] * ins[2].shape[1]
    found = [phase.collect_gains(cells) for phase in (row, column)]
    for kind in range(2):
        rounded = [member[kind].astype(bf16).astype(f32) for member in found]
        total = (rounded[0] + rounded[1]).reshape(outs[2 + kind].shape)
        outs[2 + kind][...] = total.astype(bf16)
    for copies in returning:
        arrive(copies)
    for copy in started:
        copy.wait_send()


def on_device(counts, queries, key_vectors, values, strength, decay_rate, out_grad):
    n_row, n_col = counts
    rows, cols, heads, size = queries.shape
    row_tokens, col_tokens = n_row * cols, n_col * rows
    members = jnp.stack([queries, key_vectors, values, out_grad], axis=1)
    row_source = members.reshape(rows, 4, cols * heads, size)
    members = jnp.stack([queries, key_vectors, values, out_grad], axis=0)
    col_source = jnp.transpose(members, (2, 0, 1, 3, 4)).reshape(cols, 4, rows * heads, size)

    def scratch(count, lines, span):
        held = (count, 2 * lines + -2 * lines % 16, lanes)
        table = (2 * lines * count * span // lanes, lanes)
        sems = pltpu.SemaphoreType.DMA
        return [
            pltpu.VMEM((count, lines, 4, span, size), bf16),
            pltpu.VMEM(held, bf16),
            pltpu.VMEM(held, bf16),
            pltpu.VMEM(held, bf16),
            pltpu.VMEM(held, bf16),
            pltpu.VMEM((count, lines, 3, span, size), bf16),
            pltpu.VMEM(table, f32),
            sems((lines + 1, count - 1)),
            sems((lines + 1, count - 1)),
            sems((lines + 1,)),
            sems((lines + 1, count - 1)),
            sems((lines + 1, count - 1)),
            sems((lines + 1,)),
        ]

    most = max(row_tokens, col_tokens) * heads
    shapes = [
        jax.ShapeDtypeStruct((rows, 3, cols * heads, size), bf16),
        jax.ShapeDtypeStruct((cols, 3, rows * heads, size), bf16),
        jax.ShapeDtypeStruct((rows, cols, heads), bf16),
        jax.ShapeDtypeStruct((rows, cols, heads), bf16),
    ]
    places = [pl.BlockSpec(memory_space=pl.ANY)] * 2 + [pl.BlockSpec(memory_space=pltpu.VMEM)] * 2
    row_back, col_back, strength_grad, decay_grad = pl.pallas_call(
        functools.partial(kernel, counts, heads),
        out_shape=shapes,
        in_specs=places,
        out_specs=places,
        scratch_shapes=scratch(n_row, rows // n_row, cols * heads)
        + scratch(n_col, cols // n_col, rows * heads)
        + [pltpu.VMEM((4 * most, size), f32), pltpu.VMEM((3 * most, size), f32)],
        compiler_params=pltpu.CompilerParams(
            collective_id=0, has_side_effects=True, vmem_limit_bytes=40 * 2**20
        ),
        name="exchange_and_solve",
    )(
        row_source,
        col_source,
        strength,
        decay_rate,
    )

    row_back = row_back.reshape(rows, 3, cols, heads, size)
    col_back = col_back.reshape(cols, 3, rows, heads, size)

    def merged(member):
        first = row_back[:, member].astype(f32)
        second = jnp.swapaxes(col_back[:, member], 0, 1).astype(f32)
        return (first + second).astype(bf16)

    return (merged(0), merged(1), merged(2), strength_grad, decay_grad)


def solution(mesh):
    counts = (mesh.shape["gc"], mesh.shape["gr"])
    wide = P("gr", "gc", None, None)
    narrow = P("gr", "gc", None)
    return jax.shard_map(
        functools.partial(on_device, counts),
        mesh=mesh,
        in_specs=(wide, wide, wide, narrow, narrow, wide),
        out_specs=(wide, wide, wide, narrow, narrow),
        check_vma=False,
    )
```
